32 devices in a mesh: groups: 2 (over y), blk: 4 (over z), col: 4 (over x, core).
Axes of the slice: x: 2, y: 2, z: 4, core: 2. Of those that a mesh axis runs over, the one named last changes fastest.
Arguments:
- aic: float32 [256, 32768], P(('groups', 'blk'), 'col'), parts along dimension 0, may hold values from -0.03125 to 0.03125
- downwash: float32 [8, 8192, 384], P(('groups', 'col'), 'blk'), parts along dimension 0, may hold values from -6 to 6
- node_modes: float32 [6, 32, 192], P(None, 'blk'), may hold values from -0.4375 to 0.4375
- src_rows: int32 [4, 4, 4, 8], P('blk', 'col'), may hold values from 0 to 7
- dst_nodes: int32 [4, 4, 4, 8], P('blk', 'col'), may hold values from 0 to 7
- counts: int32 [4, 4, 4], P('blk', 'col'), may hold values from 0 to 8, as said below
- spline_weights: float32 [4, 4, 6, 4, 8], P('blk', 'col'), may hold values from -0.6 to 0.6
Outputs:
- gaf: float32 [384, 384], P('groups'), parts along dimension 0
The draws below stay inside these ranges and needn't reach their ends.
There are 2 independent parts, one for each index of `groups`. The reference program is written for one: setup_inputs(seed, part) draws one part's arguments, and reference() takes and returns one part's arrays. A program takes and returns all parts, laid end to end along the dimension named above; an argument that names none is the same for every part. Nothing has to cross between parts.
Inputs may be any that keep to these rules, and one draw needn't show every extreme that they name: `counts`: slot s of a list is live when s < count; every source sub-block sends 8 live slots to its own owner, and one owner receives 8 live slots from every source sub-block. `src_rows`: rows within a sub-block of 8 rows. `dst_nodes`: nodes within an owner.
All inputs are finite; a program needn't handle non-finite values.
Results may differ from the reference program's by a relative error of at most 0.0003.
Values sent between devices are 32-bit elements; how exact they have to be, the bound alone decides.
No kernel may reach another device: no remote copies, remote signals or barrier semaphores. Data moves between devices by JAX's collectives and lax.ppermute only.
A program may use at most 64 MiB of HBM per device.

```python
import jax
import jax.numpy as jnp
from jax import lax

PANELS = 32768
MODES = 192
ROW_DEV = 32
CAP = 8
NODE_DEV = 8
ROWS = 128
PCOL = 8192
ROW_SUB = 8
NODES = 32
N_BLK = 4
N_COL = 4


def draw_counts(key, part):
    key_level = jax.random.fold_in(key, 11)
    key_count = jax.random.fold_in(key, 12)
    key_star = jax.random.fold_in(key, 13)
    level = jax.random.randint(key_level, (N_BLK,), 0, 3)
    limit = CAP * (2 + level) // 4
    drawn = jax.random.randint(key_count, (N_BLK, N_COL, N_BLK), 0, limit[None, None, :] + 1)
    star = jax.random.randint(key_star, (), 0, N_BLK)
    owner = jnp.arange(N_BLK)[None, None, :]
    source = jnp.arange(N_BLK)[:, None, None]
    full = jnp.logical_or(owner == star, owner == source)
    return jnp.where(full, CAP, drawn).astype(jnp.int32)


def touch_ends(values, stream_key, low, high):
    shape = values.shape
    spot = [jax.random.randint(jax.random.fold_in(stream_key, axis), (), 0, shape[axis]) for axis in range(len(shape))]
    values = values.at[tuple(spot)].set(low)
    longest = shape.index(max(shape))
    spot[longest] = (spot[longest] + 1) % shape[longest]
    return values.at[tuple(spot)].set(high)


def steps_of(key, extent, split, least, top_value):
    loudness, own = 1.0, jax.random.fold_in(key, 6)
    for axis_at, shards_of in split:
        heights = jnp.exp(jax.random.uniform(jax.random.fold_in(own, axis_at), (shards_of,), jnp.float32, least / len(split), top_value / len(split)))
        loudness = loudness * jnp.repeat(heights, extent[axis_at] // shards_of).reshape([-1 if axis == axis_at else 1 for axis in range(len(extent))])
    return loudness


def gaussian(stream_key, extent, width, most, pieces=(), held_as=jnp.bfloat16):
    result = width * jax.random.normal(stream_key, extent, jnp.float32)
    if pieces:
        result = result * steps_of(stream_key, extent, pieces, -0.22, 0.18)
    return jnp.clip(result, -most, most).astype(held_as)


def setup_inputs(seed: int = 0, part: int = 0) -> dict:
    arg_keys = jax.random.split(jax.random.key(seed), 8)
    part_splits = jax.random.split(jax.random.fold_in(arg_keys[7], part), 8)
    aic = gaussian(part_splits[0], (ROWS, PANELS), PANELS ** -0.5, 0.03125, ((0, 4), (1, 4)), jnp.float32)
    downwash = gaussian(part_splits[1], (N_COL, PCOL, 2 * MODES), 1.0, 6.0, ((0, 4), (1, 4)), jnp.float32)
    node_modes = gaussian(arg_keys[2], (6, NODES, MODES), (6 * NODES) ** -0.5, 0.4375, ((1, 4),), jnp.float32)
    src_rows = touch_ends(jax.random.randint(arg_keys[3], (N_BLK, N_COL, N_BLK, CAP), 0, ROW_SUB), jax.random.fold_in(arg_keys[3], 1), 0, ROW_SUB - 1).astype(jnp.int32)
    dst_nodes = touch_ends(jax.random.randint(arg_keys[4], (N_BLK, N_COL, N_BLK, CAP), 0, NODE_DEV), jax.random.fold_in(arg_keys[4], 1), 0, NODE_DEV - 1).astype(jnp.int32)
    counts = draw_counts(jax.random.fold_in(arg_keys[7], 71), part)
    spline_weights = gaussian(arg_keys[6], (N_BLK, N_COL, 6, N_BLK, CAP), 0.1, 0.6, ((0, 4), (1, 4)), jnp.float32)
    return {"aic": aic, "downwash": downwash, "node_modes": node_modes, "src_rows": src_rows, "dst_nodes": dst_nodes, "counts": counts, "spline_weights": spline_weights}


def reference(aic, downwash, node_modes, src_rows, dst_nodes, counts, spline_weights):
    flat = downwash.reshape(PANELS, 2 * MODES)
    pressure = jnp.dot(aic, flat, precision=lax.Precision.HIGHEST, preferred_element_type=jnp.float32)
    sub_base = jnp.arange(N_COL, dtype=jnp.int32)[:, None, None] * ROW_SUB
    owner_base = jnp.arange(N_BLK, dtype=jnp.int32)[None, :, None] * NODE_DEV
    slot_index = jnp.arange(CAP, dtype=jnp.int32)[None, None, :]

    def add_block(loads, block_id):
        row_ids = (block_id * ROW_DEV + sub_base + src_rows[block_id]).astype(jnp.int32)
        node_ids = (owner_base + dst_nodes[block_id]).astype(jnp.int32)
        live = (slot_index < counts[block_id][:, :, None]).astype(jnp.float32)
        forces = pressure[row_ids]
        weights = jnp.transpose(spline_weights[block_id], (0, 2, 3, 1)) * live[..., None]
        weighted = weights[..., None] * forces[:, :, :, None, :]
        loads = loads.at[node_ids.reshape(-1)].add(weighted.reshape(-1, 6, 2 * MODES))
        return loads, None

    start = jnp.zeros((NODES, 6, 2 * MODES), jnp.float32)
    loads, unused = lax.scan(add_block, start, jnp.arange(N_BLK, dtype=jnp.int32))
    return jnp.einsum("dnm,ndk->mk", node_modes, loads, precision=lax.Precision.HIGHEST)
```

```python
import jax
import jax.numpy as jnp
from jax import lax
from jax.sharding import PartitionSpec as P

HIGH = lax.Precision.HIGH


def swap(value, axis, mask):
    pairs = [(source, source ^ mask) for source in range(lax.axis_size(axis))]
    return lax.ppermute(value, axis, pairs)


def masks(axis):
    count, mask, found = lax.axis_size(axis), 1, []
    while mask < count:
        found.append(mask)
        mask *= 2
    return found


def gathered(value, axis):
    stack = value[None]
    for mask in masks(axis):
        stack = jnp.concatenate([stack, swap(stack, axis, mask)])
    return stack


def dot(left, right):
    return jnp.dot(left, right, precision=HIGH, preferred_element_type=jnp.float32)


def spline(src_rows, dst_nodes, counts, weights, sub_rows, node_count):
    slots = src_rows.shape[-1]
    live = jnp.arange(slots, dtype=jnp.int32) < counts[:, None]
    rows = jnp.arange(sub_rows, dtype=jnp.int32)[:, None, None] == src_rows
    rows = jnp.logical_and(rows, live).astype(jnp.float32)
    nodes = jnp.arange(node_count, dtype=jnp.int32)[:, None, None] == dst_nodes
    spread = weights[:, None] * nodes.astype(jnp.float32)
    matrix = jnp.sum(rows[:, None, None] * spread, axis=-1)
    return jnp.transpose(matrix, (0, 3, 1, 2)).reshape(sub_rows, -1)


def shards(aic, downwash, node_modes, src_rows, dst_nodes, counts, spline_weights):
    blk_count, col_count = lax.axis_size("blk"), lax.axis_size("col")
    blk, col = lax.axis_index("blk"), lax.axis_index("col")
    shapes = downwash[0]
    panels = shapes.shape[0]
    block_rows = aic.shape[0]
    sub_rows = block_rows // col_count
    dofs, node_count, modes = node_modes.shape

    def columns(mask):
        return lax.dynamic_slice_in_dim(aic, (blk ^ mask) * panels, panels, 1)

    order = sorted(range(1, blk_count), key=lambda mask: (mask < blk_count // 2, mask))
    arrived = {mask: swap(columns(mask), "blk", mask) for mask in order}
    arrived[0] = columns(0)
    pieces = jnp.stack([dot(arrived[mask], shapes) for mask in range(blk_count)])

    matrix = spline(
        src_rows[0, 0], dst_nodes[0, 0], counts[0, 0], spline_weights[0, 0], sub_rows, node_count
    )
    flat_modes = node_modes.reshape(dofs * node_count, modes)
    share = dofs * node_count // col_count
    modes_share = lax.dynamic_slice_in_dim(flat_modes, col * share, share, 0)
    natural_blk = blk ^ jnp.arange(blk_count, dtype=jnp.int32)
    natural_col = col ^ jnp.arange(col_count, dtype=jnp.int32)

    def everywhere(value):
        stack = gathered(gathered(value, "blk"), "col")
        return jnp.swapaxes(stack[natural_col], 0, 1)

    if matrix.shape[1] == modes:
        packed = everywhere(jnp.concatenate([modes_share, matrix]))
        all_modes = packed[natural_blk, :, :share].reshape(-1, modes)
        transfer = dot(packed[:, :, share:].reshape(-1, modes), all_modes)
    else:
        all_modes = everywhere(modes_share)[natural_blk].reshape(-1, modes)
        transfer = everywhere(dot(matrix, all_modes)).reshape(-1, modes)
    transfer = transfer.reshape(blk_count, block_rows, modes)

    half = block_rows // 2
    side = col % 2
    kept = lax.dynamic_slice_in_dim(pieces, side * half, half, 1)
    given = lax.dynamic_slice_in_dim(pieces, (1 - side) * half, half, 1)
    kept = kept + swap(given, "col", 1)
    for mask in masks("col")[1:]:
        kept = kept + swap(kept, "col", mask)
    for mask in masks("blk"):
        turned = kept[jnp.arange(blk_count) ^ mask]
        kept = kept + swap(turned, "blk", mask)
    other = swap(kept, "col", 1)
    first = lax.dynamic_slice_in_dim(transfer, side * half, half, 1)
    second = lax.dynamic_slice_in_dim(transfer, (1 - side) * half, half, 1)
    width = shapes.shape[1]
    return dot(first.reshape(-1, modes).T, kept.reshape(-1, width)) + dot(
        second.reshape(-1, modes).T, other.reshape(-1, width)
    )


def solution(mesh):
    placed = (
        P(("groups", "blk"), "col"),
        P(("groups", "col"), "blk", None),
        P(None, "blk", None),
        P("blk", "col", None, None),
        P("blk", "col", None, None),
        P("blk", "col", None),
        P("blk", "col", None, None, None),
    )
    return jax.shard_map(
        shards, mesh=mesh, in_specs=placed, out_specs=P("groups", None), check_vma=False
    )
```

```python
import functools

import jax
import jax.numpy as jnp
from jax import lax
from jax.experimental import pallas as pl
from jax.experimental.pallas import tpu as pltpu
from jax.sharding import PartitionSpec as P

HIGH = lax.Precision.HIGH
HIGHEST = lax.Precision.HIGHEST
VMEM = pl.BlockSpec(memory_space=pltpu.VMEM)
SMEM = pl.BlockSpec(memory_space=pltpu.SMEM)
ANY = pl.BlockSpec(memory_space=pl.ANY)
ROOM = pltpu.CompilerParams(vmem_limit_bytes=32 * 1024 * 1024)


def swap(value, axis, mask):
    pairs = [(source, source ^ mask) for source in range(lax.axis_size(axis))]
    return lax.ppermute(value, axis, pairs)


def masks(axis):
    count, mask, found = lax.axis_size(axis), 1, []
    while mask < count:
        found.append(mask)
        mask *= 2
    return found


def gathered(value, axis):
    stack = value[None]
    for mask in masks(axis):
        stack = jnp.concatenate([stack, swap(stack, axis, mask)])
    return stack


def dot(left, right):
    return jnp.dot(left, right, precision=HIGH, preferred_element_type=jnp.float32)


def spline(src_rows, dst_nodes, counts, weights, sub_rows, node_count):
    slots = src_rows.shape[-1]
    live = jnp.arange(slots, dtype=jnp.int32) < counts[:, None]
    rows = jnp.arange(sub_rows, dtype=jnp.int32)[:, None, None] == src_rows
    rows = jnp.logical_and(rows, live).astype(jnp.float32)
    nodes = jnp.arange(node_count, dtype=jnp.int32)[:, None, None] == dst_nodes
    spread = weights[:, None] * nodes.astype(jnp.float32)
    matrix = jnp.sum(rows[:, None, None] * spread, axis=-1)
    return jnp.transpose(matrix, (0, 3, 1, 2)).reshape(sub_rows, -1)


def by_parts(aic, downwash, node_modes, src_rows, dst_nodes, counts, spline_weights):
    blk_count, col_count = lax.axis_size("blk"), lax.axis_size("col")
    blk, col = lax.axis_index("blk"), lax.axis_index("col")
    shapes = downwash[0]
    panels = shapes.shape[0]
    block_rows = aic.shape[0]
    sub_rows = block_rows // col_count
    dofs, node_count, modes = node_modes.shape

    def columns(mask):
        return lax.dynamic_slice_in_dim(aic, (blk ^ mask) * panels, panels, 1)

    order = sorted(range(1, blk_count), key=lambda mask: (mask < blk_count // 2, mask))
    arrived = {mask: swap(columns(mask), "blk", mask) for mask in order}
    arrived[0] = columns(0)
    pieces = jnp.stack([dot(arrived[mask], shapes) for mask in range(blk_count)])

    matrix = spline(
        src_rows[0, 0], dst_nodes[0, 0], counts[0, 0], spline_weights[0, 0], sub_rows, node_count
    )
    flat_modes = node_modes.reshape(dofs * node_count, modes)
    share = dofs * node_count // col_count
    modes_share = lax.dynamic_slice_in_dim(flat_modes, col * share, share, 0)
    natural_blk = blk ^ jnp.arange(blk_count, dtype=jnp.int32)
    natural_col = col ^ jnp.arange(col_count, dtype=jnp.int32)

    def everywhere(value):
        stack = gathered(gathered(value, "blk"), "col")
        return jnp.swapaxes(stack[natural_col], 0, 1)

    if matrix.shape[1] == modes:
        packed = everywhere(jnp.concatenate([modes_share, matrix]))
        all_modes = packed[natural_blk, :, :share].reshape(-1, modes)
        transfer = dot(packed[:, :, share:].reshape(-1, modes), all_modes)
    else:
        all_modes = everywhere(modes_share)[natural_blk].reshape(-1, modes)
        transfer = everywhere(dot(matrix, all_modes)).reshape(-1, modes)
    transfer = transfer.reshape(blk_count, block_rows, modes)

    half = block_rows // 2
    side = col % 2
    kept = lax.dynamic_slice_in_dim(pieces, side * half, half, 1)
    given = lax.dynamic_slice_in_dim(pieces, (1 - side) * half, half, 1)
    kept = kept + swap(given, "col", 1)
    for mask in masks("col")[1:]:
        kept = kept + swap(kept, "col", mask)
    for mask in masks("blk"):
        turned = kept[jnp.arange(blk_count) ^ mask]
        kept = kept + swap(turned, "blk", mask)
    other = swap(kept, "col", 1)
    first = lax.dynamic_slice_in_dim(transfer, side * half, half, 1)
    second = lax.dynamic_slice_in_dim(transfer, (1 - side) * half, half, 1)
    width = shapes.shape[1]
    return dot(first.reshape(-1, modes).T, kept.reshape(-1, width)) + dot(
        second.reshape(-1, modes).T, other.reshape(-1, width)
    )


def cost(microseconds):
    return pl.CostEstimate(flops=0, bytes_accessed=int(microseconds * 3.5e6), transcendentals=0)


def after(value, *others):
    return lax.optimization_barrier((value, *others))[0]


def f32(*shape):
    return jax.ShapeDtypeStruct(shape, jnp.float32)


def cut_kernel(pieces, aic, *refs):
    outs, sems = refs[:-1], refs[-1]
    blk = lax.axis_index("blk")
    copies = []
    for at, (mask, first, rows) in enumerate(pieces):
        panels = outs[at].shape[1]
        start = pl.multiple_of((blk ^ mask) * panels, 128)
        source = aic.at[pl.ds(first, rows), pl.ds(start, panels)]
        copies.append(pltpu.make_async_copy(source, outs[at], sems.at[at]))
        copies[-1].start()
    for copy in copies:
        copy.wait()


def cut_out(aic, panels, pieces):
    return pl.pallas_call(
        functools.partial(cut_kernel, pieces),
        out_shape=[f32(rows, panels) for _, _, rows in pieces],
        in_specs=[ANY],
        out_specs=[VMEM] * len(pieces),
        scratch_shapes=[pltpu.SemaphoreType.DMA((len(pieces),))],
        cost_estimate=cost(2),
    )(aic)


def spline_kernel(src_rows, dst_nodes, counts, weights, modes, pack):
    owners, slots = src_rows.shape[2:]
    dofs, node_count, width = modes.shape
    sub_rows = pack.shape[0] - dofs * node_count // lax.axis_size("col")
    shape = (sub_rows, owners * dofs * node_count)
    row = lax.broadcasted_iota(jnp.int32, shape, 0)
    place = lax.broadcasted_iota(jnp.int32, shape, 1)
    total = jnp.zeros(shape, jnp.float32)
    for owner in range(owners):
        live = counts[0, 0, owner]
        for slot in range(slots):
            node = owner * dofs * node_count + dst_nodes[0, 0, owner, slot]
            term = jnp.zeros(shape, jnp.float32)
            for dof in range(dofs):
                term = jnp.where(place == node + dof * node_count, weights[0, 0, dof, owner, slot], term)
            here = jnp.where(slot < live, src_rows[0, 0, owner, slot], -1)
            total = total + jnp.where(row == here, term, 0.0)
    pack[:sub_rows, :] = total
    flat = modes[...].reshape(dofs * node_count, width)
    share = dofs * node_count // lax.axis_size("col")
    col = lax.axis_index("col")
    for turn in range(lax.axis_size("col")):

        @pl.when(col == turn)
        def _():
            pack[sub_rows:, :] = flat[turn * share : (turn + 1) * share]


def transfer_kernel(sub_rows, packs, high, low, modes, spread):
    cols, blk_count = packs.shape[:2]
    blk, col = lax.axis_index("blk"), lax.axis_index("col")
    share = packs.shape[2] - sub_rows
    half = blk_count // 2
    quarter = cols // 2
    own = blk // half * half
    bits = cols.bit_length() - 1

    def entry(place):
        mask = col ^ place
        return sum(((mask >> bit) & 1) << (bits - 1 - bit) for bit in range(bits))

    for b in range(blk_count):
        for c in range(cols):
            at = (b * cols + c) * share
            modes[at : at + share, :] = packs[entry(c), blk ^ b, sub_rows:, :]
    at = 0
    for turn in range(2):
        for b in range(blk_count):
            block = own + b if b < half else half - own + b - half
            for c in range(quarter):
                place = (lax.rem(col, 2) ^ turn) * quarter + c
                spread[at : at + sub_rows, :] = packs[entry(place), blk ^ block, :sub_rows, :]
                at += sub_rows
    whole = lax.dot_general(
        modes[...], spread[...], (((0,), (1,)), ((), ())), precision=HIGHEST,
        preferred_element_type=jnp.float32,
    )
    high[...], low[...] = split(whole)


def last_kernel(high, low, total, other, out):
    right_high, right_low = split(jnp.concatenate([total[...], other[...]]))
    out[...] = mxu(high[...], right_high) + (mxu(high[...], right_low) + mxu(low[...], right_high))


def split(value):
    high = value.astype(jnp.bfloat16)
    return high, (value - high.astype(jnp.float32)).astype(jnp.bfloat16)


def mxu(left, right):
    return jnp.dot(left, right, preferred_element_type=jnp.float32)


def halves_kernel(shapes, high, low, buffer, sems):
    steps = buffer.shape[0]
    rows = buffer.shape[1]
    copies = [
        pltpu.make_async_copy(shapes.at[pl.ds(step * rows, rows), :], buffer.at[step], sems.at[step])
        for step in range(steps)
    ]
    for copy in copies:
        copy.start()
    for step, copy in enumerate(copies):
        copy.wait()
        at = pl.ds(step * rows, rows)
        high[at, :], low[at, :] = split(buffer[step])


def halves(shapes, steps):
    rows = shapes.shape[0] // steps
    return pl.pallas_call(
        halves_kernel,
        out_shape=[jax.ShapeDtypeStruct(shapes.shape, jnp.bfloat16)] * 2,
        in_specs=[ANY],
        out_specs=[VMEM] * 2,
        scratch_shapes=[
            pltpu.VMEM((steps, rows, shapes.shape[1]), jnp.float32),
            pltpu.SemaphoreType.DMA((steps,)),
        ],
        compiler_params=ROOM,
        cost_estimate=cost(1),
    )(shapes)


def product(pieces, high, low):
    rows = [split(piece[...]) for piece in pieces]
    left_high = jnp.concatenate([r[0] for r in rows])
    left_low = jnp.concatenate([r[1] for r in rows])
    size = left_high.shape[0]
    both = mxu(jnp.concatenate([left_high, left_low]), high[...])
    return both[:size] + both[size:] + mxu(left_high, low[...])


def early_kernel(*refs):
    *pieces, high, low, out = refs
    out[...] = product(pieces, high, low).reshape(out.shape)


def late_kernel(groups, *refs):
    *pieces, early, high, low, kept, given, total = refs
    done = early.shape[0]
    total[:done] = early[...]
    total[done:] = product(pieces, high, low).reshape(total[done:].shape)
    blk, core = lax.axis_index("blk"), lax.rem(lax.axis_index("col"), 2)
    half = total.shape[1] // 2
    at = first = 0
    for group in groups:
        for index in range(group):
            source = first + ((blk & (group - 1)) ^ index)
            kept[at : at + half, :] = total[source, pl.ds(pl.multiple_of(core * half, 8), half), :]
            given[at : at + half, :] = total[source, pl.ds(pl.multiple_of((1 - core) * half, 8), half), :]
            at += half
        first += group


def early_products(pieces, high, low):
    return pl.pallas_call(
        early_kernel,
        out_shape=f32(len(pieces), pieces[0].shape[0], high.shape[1]),
        in_specs=[VMEM] * (len(pieces) + 2),
        out_specs=VMEM,
        compiler_params=ROOM,
        cost_estimate=cost(1),
    )(*pieces, high, low)


def late_products(groups, pieces, early, high, low):
    count, (rows, width) = sum(groups), early.shape[1:]
    return pl.pallas_call(
        functools.partial(late_kernel, groups),
        out_shape=[f32(rows * count // 2, width)] * 2,
        in_specs=[VMEM] * (len(pieces) + 3),
        out_specs=[VMEM] * 2,
        scratch_shapes=[pltpu.VMEM((count, rows, width), jnp.float32)],
        compiler_params=ROOM,
        cost_estimate=cost(0.1),
    )(*pieces, early, high, low)


def shards(aic, downwash, node_modes, src_rows, dst_nodes, counts, spline_weights):
    blk_count, col_count = lax.axis_size("blk"), lax.axis_size("col")
    shapes = downwash[0]
    panels, width = shapes.shape
    block_rows = aic.shape[0]
    sub_rows = block_rows // col_count
    dofs, node_count, modes = node_modes.shape
    loads = blk_count * dofs * node_count
    half = blk_count // 2

    share = dofs * node_count // col_count
    blk = lax.axis_index("blk")

    def columns(mask, source=aic):
        return lax.dynamic_slice_in_dim(source, (blk ^ mask) * panels, panels, 1)

    far_masks = list(range(half, blk_count))
    near = [columns(mask) for mask in range(1, half)]
    far = [columns(mask) for mask in far_masks]
    rest, lists, shapes, *cuts = lax.optimization_barrier((aic, src_rows, shapes, *near, *far))
    near, far = cuts[: half - 1], cuts[half - 1 :]
    near = [swap(piece, "blk", mask + 1) for mask, piece in enumerate(near)]
    far[:-1] = [swap(piece, "blk", mask) for mask, piece in zip(far_masks, far[:-1])]
    near = [columns(0, rest), *near]
    high, low = halves(shapes, 4)

    pack = pl.pallas_call(
        spline_kernel,
        out_shape=f32(sub_rows + share, modes),
        in_specs=[SMEM] * 4 + [VMEM],
        out_specs=VMEM,
        cost_estimate=cost(1),
    )(lists, dst_nodes, counts, spline_weights, node_modes)
    far[-1] = swap(after(far[-1], pack), "blk", far_masks[-1])
    packs = [pack] + [swap(pack, "blk", mask) for mask in range(1, blk_count)]
    waiting = lax.optimization_barrier((*packs, *near, *far[:-1]))
    packs, near, far[:-1] = waiting[:blk_count], waiting[blk_count : blk_count + half], waiting[blk_count + half :]
    packs = jnp.stack(packs)[None]
    col_masks = masks("col")
    for mask in col_masks[:0:-1]:
        packs = jnp.concatenate([packs, swap(packs, "col", mask)])
    packs, high = lax.optimization_barrier((packs, high))
    early = early_products([*near, *far[:-1]], high, low)
    total, given = late_products((half, half), far[-1:], early, high, low)
    packs = jnp.concatenate([packs, swap(packs, "col", 1)])
    given = swap(given, "col", 1)
    total = total + given
    for mask in masks("col")[1:]:
        total = total + swap(total, "col", mask)
    for mask in masks("blk")[:-1]:
        total = total + swap(total, "blk", mask)
    there = swap(total, "blk", half)
    transfer = pl.pallas_call(
        functools.partial(transfer_kernel, sub_rows),
        out_shape=[jax.ShapeDtypeStruct((modes, blk_count * block_rows), jnp.bfloat16)] * 2,
        in_specs=[VMEM],
        out_specs=[VMEM] * 2,
        scratch_shapes=[
            pltpu.VMEM((loads, modes), jnp.float32),
            pltpu.VMEM((blk_count * block_rows, loads), jnp.float32),
        ],
        cost_estimate=cost(3),
    )(packs)
    there, *transfer = lax.optimization_barrier((there, *transfer))
    rows = total.shape[0] // 2
    total = total + jnp.concatenate([there[rows:], there[:rows]])
    other = swap(total, "col", 1)
    return pl.pallas_call(
        last_kernel,
        out_shape=f32(modes, width),
        in_specs=[VMEM] * 4,
        compiler_params=ROOM,
    )(*transfer, total, other)


def solution(mesh):
    placed = (
        P(("groups", "blk"), "col"),
        P(("groups", "col"), "blk", None),
        P(None, "blk", None),
        P("blk", "col", None, None),
        P("blk", "col", None, None),
        P("blk", "col", None),
        P("blk", "col", None, None, None),
    )

    def program(*arrays):
        dofs, nodes, modes = arrays[2].shape
        body = shards if dofs * nodes == modes else by_parts
        return jax.shard_map(
            body, mesh=mesh, in_specs=placed, out_specs=P("groups", None), check_vma=False
        )(*arrays)

    return program
```

```python
import functools

import jax
import jax.numpy as jnp
from jax import lax
from jax.experimental import pallas as pl
from jax.experimental.pallas import tpu as pltpu
from jax.sharding import PartitionSpec as P

HIGH = lax.Precision.HIGH
HIGHEST = lax.Precision.HIGHEST
VMEM = pl.BlockSpec(memory_space=pltpu.VMEM)
SMEM = pl.BlockSpec(memory_space=pltpu.SMEM)
ANY = pl.BlockSpec(memory_space=pl.ANY)
ROOM = pltpu.CompilerParams(vmem_limit_bytes=32 * 1024 * 1024)


def swap(value, axis, mask):
    pairs = [(source, source ^ mask) for source in range(lax.axis_size(axis))]
    return lax.ppermute(value, axis, pairs)


def masks(axis):
    count, mask, found = lax.axis_size(axis), 1, []
    while mask < count:
        found.append(mask)
        mask *= 2
    return found


def gathered(value, axis):
    stack = value[None]
    for mask in masks(axis):
        stack = jnp.concatenate([stack, swap(stack, axis, mask)])
    return stack


def dot(left, right):
    return jnp.dot(left, right, precision=HIGH, preferred_element_type=jnp.float32)


def spline(src_rows, dst_nodes, counts, weights, sub_rows, node_count):
    slots = src_rows.shape[-1]
    live = jnp.arange(slots, dtype=jnp.int32) < counts[:, None]
    rows = jnp.arange(sub_rows, dtype=jnp.int32)[:, None, None] == src_rows
    rows = jnp.logical_and(rows, live).astype(jnp.float32)
    nodes = jnp.arange(node_count, dtype=jnp.int32)[:, None, None] == dst_nodes
    spread = weights[:, None] * nodes.astype(jnp.float32)
    matrix = jnp.sum(rows[:, None, None] * spread, axis=-1)
    return jnp.transpose(matrix, (0, 3, 1, 2)).reshape(sub_rows, -1)


def by_parts(aic, downwash, node_modes, src_rows, dst_nodes, counts, spline_weights):
    blk_count, col_count = lax.axis_size("blk"), lax.axis_size("col")
    blk, col = lax.axis_index("blk"), lax.axis_index("col")
    shapes = downwash[0]
    panels = shapes.shape[0]
    block_rows = aic.shape[0]
    sub_rows = block_rows // col_count
    dofs, node_count, modes = node_modes.shape

    def columns(mask):
        return lax.dynamic_slice_in_dim(aic, (blk ^ mask) * panels, panels, 1)

    order = sorted(range(1, blk_count), key=lambda mask: (mask < blk_count // 2, mask))
    arrived = {mask: swap(columns(mask), "blk", mask) for mask in order}
    arrived[0] = columns(0)
    pieces = jnp.stack([dot(arrived[mask], shapes) for mask in range(blk_count)])

    matrix = spline(
        src_rows[0, 0], dst_nodes[0, 0], counts[0, 0], spline_weights[0, 0], sub_rows, node_count
    )
    flat_modes = node_modes.reshape(dofs * node_count, modes)
    share = dofs * node_count // col_count
    modes_share = lax.dynamic_slice_in_dim(flat_modes, col * share, share, 0)
    natural_blk = blk ^ jnp.arange(blk_count, dtype=jnp.int32)
    natural_col = col ^ jnp.arange(col_count, dtype=jnp.int32)

    def everywhere(value):
        stack = gathered(gathered(value, "blk"), "col")
        return jnp.swapaxes(stack[natural_col], 0, 1)

    if matrix.shape[1] == modes:
        packed = everywhere(jnp.concatenate([modes_share, matrix]))
        all_modes = packed[natural_blk, :, :share].reshape(-1, modes)
        transfer = dot(packed[:, :, share:].reshape(-1, modes), all_modes)
    else:
        all_modes = everywhere(modes_share)[natural_blk].reshape(-1, modes)
        transfer = everywhere(dot(matrix, all_modes)).reshape(-1, modes)
    transfer = transfer.reshape(blk_count, block_rows, modes)

    half = block_rows // 2
    side = col % 2
    kept = lax.dynamic_slice_in_dim(pieces, side * half, half, 1)
    given = lax.dynamic_slice_in_dim(pieces, (1 - side) * half, half, 1)
    kept = kept + swap(given, "col", 1)
    for mask in masks("col")[1:]:
        kept = kept + swap(kept, "col", mask)
    for mask in masks("blk"):
        turned = kept[jnp.arange(blk_count) ^ mask]
        kept = kept + swap(turned, "blk", mask)
    other = swap(kept, "col", 1)
    first = lax.dynamic_slice_in_dim(transfer, side * half, half, 1)
    second = lax.dynamic_slice_in_dim(transfer, (1 - side) * half, half, 1)
    width = shapes.shape[1]
    return dot(first.reshape(-1, modes).T, kept.reshape(-1, width)) + dot(
        second.reshape(-1, modes).T, other.reshape(-1, width)
    )


def cost(microseconds):
    return pl.CostEstimate(flops=0, bytes_accessed=int(microseconds * 3.5e6), transcendentals=0)


def after(value, *others):
    return lax.optimization_barrier((value, *others))[0]


def f32(*shape):
    return jax.ShapeDtypeStruct(shape, jnp.float32)


def folded(rows):
    return rows + rows // 2


def fold(value, out, start):
    rows, width = value.shape
    wide, half = 2 * width // 3, rows // 2
    below = start + rows
    out[start:below, :] = value[:, :wide]
    out[below : below + half, : wide // 2] = value[:half, wide:]
    out[below : below + half, wide // 2 :] = value[half:, wide:]


def unfold(value, out, start):
    rows, wide = value.shape[0] * 2 // 3, value.shape[1]
    middle, end = start + rows // 2, start + rows
    out[start:end, :wide] = value[:rows]
    out[start:middle, wide:] = value[rows:, : wide // 2]
    out[middle:end, wide:] = value[rows:, wide // 2 :]


def spline_kernel(src_rows, dst_nodes, counts, weights, modes, pack):
    owners, slots = src_rows.shape[2:]
    dofs, node_count, width = modes.shape
    share = dofs * node_count // lax.axis_size("col")
    sub_rows = (pack.shape[0] - folded(share)) * 2 // 3
    shape = (sub_rows, owners * dofs * node_count)
    row = lax.broadcasted_iota(jnp.int32, shape, 0)
    place = lax.broadcasted_iota(jnp.int32, shape, 1)
    total = jnp.zeros(shape, jnp.float32)
    for owner in range(owners):
        live = counts[0, 0, owner]
        for slot in range(slots):
            node = owner * dofs * node_count + dst_nodes[0, 0, owner, slot]
            term = jnp.zeros(shape, jnp.float32)
            for dof in range(dofs):
                term = jnp.where(place == node + dof * node_count, weights[0, 0, dof, owner, slot], term)
            here = jnp.where(slot < live, src_rows[0, 0, owner, slot], -1)
            total = total + jnp.where(row == here, term, 0.0)
    fold(total, pack, 0)
    flat = modes[...].reshape(dofs * node_count, width)
    col = lax.axis_index("col")
    for turn in range(lax.axis_size("col")):

        @pl.when(col == turn)
        def _():
            fold(flat[turn * share : (turn + 1) * share], pack, folded(sub_rows))


def transfer_kernel(sub_rows, packs, high, low, modes, spread):
    cols, blk_count = packs.shape[:2]
    blk, col = lax.axis_index("blk"), lax.axis_index("col")
    spline_rows = folded(sub_rows)
    share = (packs.shape[2] - spline_rows) * 2 // 3
    half = blk_count // 2
    quarter = cols // 2
    own = blk // half * half
    bits = cols.bit_length() - 1

    def entry(place):
        mask = col ^ place
        return sum(((mask >> bit) & 1) << (bits - 1 - bit) for bit in range(bits))

    for b in range(blk_count):
        for c in range(cols):
            at = (b * cols + c) * share
            unfold(packs[entry(c), blk ^ b, spline_rows:, :], modes, at)
    at = 0
    for turn in range(2):
        for b in range(blk_count):
            block = own + b if b < half else half - own + b - half
            for c in range(quarter):
                place = (lax.rem(col, 2) ^ turn) * quarter + c
                unfold(packs[entry(place), blk ^ block, :spline_rows, :], spread, at)
                at += sub_rows
    whole = lax.dot_general(
        modes[...], spread[...], (((0,), (1,)), ((), ())), precision=HIGHEST,
        preferred_element_type=jnp.float32,
    )
    high[...], low[...] = split(whole)


def last_kernel(high, low, total, other, out):
    right_high, right_low = split(jnp.concatenate([total[...], other[...]]))
    out[...] = mxu(high[...], right_high) + (mxu(high[...], right_low) + mxu(low[...], right_high))


def split(value):
    high = value.astype(jnp.bfloat16)
    return high, (value - high.astype(jnp.float32)).astype(jnp.bfloat16)


def mxu(left, right):
    return jnp.dot(left, right, preferred_element_type=jnp.float32)


def halves_kernel(shapes, high, low, buffer, sems):
    steps = buffer.shape[0]
    rows = buffer.shape[1]
    copies = [
        pltpu.make_async_copy(shapes.at[pl.ds(step * rows, rows), :], buffer.at[step], sems.at[step])
        for step in range(steps)
    ]
    for copy in copies:
        copy.start()
    for step, copy in enumerate(copies):
        copy.wait()
        at = pl.ds(step * rows, rows)
        high[at, :], low[at, :] = split(buffer[step])


def halves(shapes, steps):
    rows = shapes.shape[0] // steps
    return pl.pallas_call(
        halves_kernel,
        out_shape=[jax.ShapeDtypeStruct(shapes.shape, jnp.bfloat16)] * 2,
        in_specs=[ANY],
        out_specs=[VMEM] * 2,
        scratch_shapes=[
            pltpu.VMEM((steps, rows, shapes.shape[1]), jnp.float32),
            pltpu.SemaphoreType.DMA((steps,)),
        ],
        compiler_params=ROOM,
        cost_estimate=cost(0.001),
    )(shapes)


def product(pieces, high, low):
    rows = [split(piece[...]) for piece in pieces]
    left_high = jnp.concatenate([r[0] for r in rows])
    left_low = jnp.concatenate([r[1] for r in rows])
    size = left_high.shape[0]
    both = mxu(jnp.concatenate([left_high, left_low]), high[...])
    return both[:size] + both[size:] + mxu(left_high, low[...])


def early_kernel(*refs):
    *pieces, high, low, out = refs
    out[...] = product(pieces, high, low)


def late_kernel(groups, *refs):
    *pieces, early, high, low, kept, given, total = refs
    done = early.shape[0]
    total[:done, :] = early[...]
    total[done:, :] = product(pieces, high, low)
    blk, core = lax.axis_index("blk"), lax.rem(lax.axis_index("col"), 2)
    rows = total.shape[0] // sum(groups)
    half = rows // 2
    at = first = 0
    for group in groups:
        for index in range(group):
            source = (first + ((blk & (group - 1)) ^ index)) * rows
            for side, out in ((core, kept), (1 - core, given)):
                place = pl.multiple_of(source + side * half, 8)
                out[at : at + half, :] = total[pl.ds(place, half), :]
            at += half
        first += group


def early_products(pieces, high, low):
    return pl.pallas_call(
        early_kernel,
        out_shape=f32(sum(piece.shape[0] for piece in pieces), high.shape[1]),
        in_specs=[VMEM] * (len(pieces) + 2),
        out_specs=VMEM,
        compiler_params=ROOM,
        cost_estimate=cost(0.001),
    )(*pieces, high, low)


def late_products(groups, pieces, early, high, low):
    width = high.shape[1]
    rows = early.shape[0] + sum(piece.shape[0] for piece in pieces)
    return pl.pallas_call(
        functools.partial(late_kernel, groups),
        out_shape=[f32(rows // 2, width)] * 2,
        in_specs=[VMEM] * (len(pieces) + 3),
        out_specs=[VMEM] * 2,
        scratch_shapes=[pltpu.VMEM((rows, width), jnp.float32)],
        compiler_params=ROOM,
        cost_estimate=cost(0.001),
    )(*pieces, early, high, low)


def joined_kernel(*refs):
    *parts, out = refs
    for index, part in enumerate(parts):
        out[index] = part[...]


def joined(*parts):
    return pl.pallas_call(
        joined_kernel,
        out_shape=f32(len(parts), *parts[0].shape),
        in_specs=[VMEM] * len(parts),
        out_specs=VMEM,
        compiler_params=ROOM,
        cost_estimate=cost(0.001),
    )(*parts)


def shards(aic, downwash, node_modes, src_rows, dst_nodes, counts, spline_weights):
    blk_count, col_count = lax.axis_size("blk"), lax.axis_size("col")
    shapes = downwash[0]
    panels, width = shapes.shape
    block_rows = aic.shape[0]
    sub_rows = block_rows // col_count
    dofs, node_count, modes = node_modes.shape
    loads = blk_count * dofs * node_count
    half = blk_count // 2

    share = dofs * node_count // col_count
    blk = lax.axis_index("blk")

    def columns(mask, source=aic):
        return lax.dynamic_slice_in_dim(source, (blk ^ mask) * panels, panels, 1)

    far_masks = list(range(half, blk_count))
    far = [columns(mask) for mask in far_masks[:-1]]
    rest, *far = lax.optimization_barrier((aic, *far))
    far = [swap(piece, "blk", mask) for mask, piece in zip(far_masks, far)]
    near = [columns(mask, rest) for mask in range(1, half)]
    last = columns(far_masks[-1], rest)
    rest, lists, shapes, last, *near = lax.optimization_barrier((rest, src_rows, shapes, last, *near))
    near = [swap(piece, "blk", mask + 1) for mask, piece in enumerate(near)]
    near = [columns(0, rest), *near]
    high, low = halves(shapes, 4)

    pack = pl.pallas_call(
        spline_kernel,
        out_shape=f32(folded(sub_rows) + folded(share), 2 * modes // 3),
        in_specs=[SMEM] * 4 + [VMEM],
        out_specs=VMEM,
        compiler_params=ROOM,
        cost_estimate=cost(0.001),
    )(lists, dst_nodes, counts, spline_weights, node_modes)
    last = swap(after(last, pack), "blk", far_masks[-1])
    packs = [pack] + [swap(pack, "blk", mask) for mask in range(1, blk_count)]
    waiting = lax.optimization_barrier((*packs, *near, *far))
    packs, near, far = waiting[:blk_count], waiting[blk_count : blk_count + half], waiting[blk_count + half :]
    packs = joined(*packs)[None]
    for mask in masks("col")[:0:-1]:
        packs = joined(packs, swap(packs, "col", mask)).reshape(-1, *packs.shape[1:])
    packs, high = lax.optimization_barrier((packs, high))

    early = early_products([*near, *far], high, low)
    total, given = late_products((half, half), [last], early, high, low)
    packs = jnp.concatenate([packs, swap(packs, "col", 1)])
    total = total + swap(given, "col", 1)
    for mask in masks("col")[1:]:
        total = total + swap(total, "col", mask)
    for mask in masks("blk")[:-1]:
        total = total + swap(total, "blk", mask)
    there = swap(total, "blk", half)
    transfer = pl.pallas_call(
        functools.partial(transfer_kernel, sub_rows),
        out_shape=[jax.ShapeDtypeStruct((modes, blk_count * block_rows), jnp.bfloat16)] * 2,
        in_specs=[VMEM],
        out_specs=[VMEM] * 2,
        scratch_shapes=[
            pltpu.VMEM((loads, modes), jnp.float32),
            pltpu.VMEM((blk_count * block_rows, loads), jnp.float32),
        ],
        compiler_params=ROOM,
        cost_estimate=cost(3),
    )(packs)
    there, *transfer = lax.optimization_barrier((there, *transfer))
    rows = total.shape[0] // 2
    total = total + jnp.concatenate([there[rows:], there[:rows]])
    other = swap(total, "col", 1)
    return pl.pallas_call(
        last_kernel,
        out_shape=f32(modes, width),
        compiler_params=ROOM,
    )(*transfer, total, other)


def solution(mesh):
    placed = (
        P(("groups", "blk"), "col"),
        P(("groups", "col"), "blk", None),
        P(None, "blk", None),
        P("blk", "col", None, None),
        P("blk", "col", None, None),
        P("blk", "col", None),
        P("blk", "col", None, None, None),
    )

    def program(*arrays):
        dofs, nodes, modes = arrays[2].shape
        blk_count, col_count = mesh.shape["blk"], mesh.shape["col"]
        small = dofs * nodes == modes and modes % 3 == 0
        body = shards if small and blk_count > 2 and col_count > 2 else by_parts
        return jax.shard_map(
            body, mesh=mesh, in_specs=placed, out_specs=P("groups", None), check_vma=False
        )(*arrays)

    return program
```

```python
import functools

import jax
import jax.numpy as jnp
from jax import lax
from jax.experimental import pallas as pl
from jax.experimental.pallas import tpu as pltpu
from jax.sharding import PartitionSpec as P

HIGH = lax.Precision.HIGH
HIGHEST = lax.Precision.HIGHEST
VMEM = pl.BlockSpec(memory_space=pltpu.VMEM)
SMEM = pl.BlockSpec(memory_space=pltpu.SMEM)
ANY = pl.BlockSpec(memory_space=pl.ANY)
ROOM = pltpu.CompilerParams(vmem_limit_bytes=32 * 1024 * 1024)


def swap(value, axis, mask):
    pairs = [(source, source ^ mask) for source in range(lax.axis_size(axis))]
    return lax.ppermute(value, axis, pairs)


def masks(axis):
    count, mask, found = lax.axis_size(axis), 1, []
    while mask < count:
        found.append(mask)
        mask *= 2
    return found


def gathered(value, axis):
    stack = value[None]
    for mask in masks(axis):
        stack = jnp.concatenate([stack, swap(stack, axis, mask)])
    return stack


def dot(left, right):
    return jnp.dot(left, right, precision=HIGH, preferred_element_type=jnp.float32)


def spline(src_rows, dst_nodes, counts, weights, sub_rows, node_count):
    slots = src_rows.shape[-1]
    live = jnp.arange(slots, dtype=jnp.int32) < counts[:, None]
    rows = jnp.arange(sub_rows, dtype=jnp.int32)[:, None, None] == src_rows
    rows = jnp.logical_and(rows, live).astype(jnp.float32)
    nodes = jnp.arange(node_count, dtype=jnp.int32)[:, None, None] == dst_nodes
    spread = weights[:, None] * nodes.astype(jnp.float32)
    matrix = jnp.sum(rows[:, None, None] * spread, axis=-1)
    return jnp.transpose(matrix, (0, 3, 1, 2)).reshape(sub_rows, -1)


def by_parts(aic, downwash, node_modes, src_rows, dst_nodes, counts, spline_weights):
    blk_count, col_count = lax.axis_size("blk"), lax.axis_size("col")
    blk, col = lax.axis_index("blk"), lax.axis_index("col")
    shapes = downwash[0]
    panels = shapes.shape[0]
    block_rows = aic.shape[0]
    sub_rows = block_rows // col_count
    dofs, node_count, modes = node_modes.shape

    def columns(mask):
        return lax.dynamic_slice_in_dim(aic, (blk ^ mask) * panels, panels, 1)

    order = sorted(range(1, blk_count), key=lambda mask: (mask < blk_count // 2, mask))
    arrived = {mask: swap(columns(mask), "blk", mask) for mask in order}
    arrived[0] = columns(0)
    pieces = jnp.stack([dot(arrived[mask], shapes) for mask in range(blk_count)])

    matrix = spline(
        src_rows[0, 0], dst_nodes[0, 0], counts[0, 0], spline_weights[0, 0], sub_rows, node_count
    )
    flat_modes = node_modes.reshape(dofs * node_count, modes)
    share = dofs * node_count // col_count
    modes_share = lax.dynamic_slice_in_dim(flat_modes, col * share, share, 0)
    natural_blk = blk ^ jnp.arange(blk_count, dtype=jnp.int32)
    natural_col = col ^ jnp.arange(col_count, dtype=jnp.int32)

    def everywhere(value):
        stack = gathered(gathered(value, "blk"), "col")
        return jnp.swapaxes(stack[natural_col], 0, 1)

    if matrix.shape[1] == modes:
        packed = everywhere(jnp.concatenate([modes_share, matrix]))
        all_modes = packed[natural_blk, :, :share].reshape(-1, modes)
        transfer = dot(packed[:, :, share:].reshape(-1, modes), all_modes)
    else:
        all_modes = everywhere(modes_share)[natural_blk].reshape(-1, modes)
        transfer = everywhere(dot(matrix, all_modes)).reshape(-1, modes)
    transfer = transfer.reshape(blk_count, block_rows, modes)

    half = block_rows // 2
    side = col % 2
    kept = lax.dynamic_slice_in_dim(pieces, side * half, half, 1)
    given = lax.dynamic_slice_in_dim(pieces, (1 - side) * half, half, 1)
    kept = kept + swap(given, "col", 1)
    for mask in masks("col")[1:]:
        kept = kept + swap(kept, "col", mask)
    for mask in masks("blk"):
        turned = kept[jnp.arange(blk_count) ^ mask]
        kept = kept + swap(turned, "blk", mask)
    other = swap(kept, "col", 1)
    first = lax.dynamic_slice_in_dim(transfer, side * half, half, 1)
    second = lax.dynamic_slice_in_dim(transfer, (1 - side) * half, half, 1)
    width = shapes.shape[1]
    return dot(first.reshape(-1, modes).T, kept.reshape(-1, width)) + dot(
        second.reshape(-1, modes).T, other.reshape(-1, width)
    )


def cost(microseconds):
    return pl.CostEstimate(flops=0, bytes_accessed=int(microseconds * 3.5e6), transcendentals=0)


def after(value, *others):
    return lax.optimization_barrier((value, *others))[0]


def f32(*shape):
    return jax.ShapeDtypeStruct(shape, jnp.float32)


def folded(rows):
    return rows + rows // 2


def fold(value, out, start):
    rows, width = value.shape
    wide, half = 2 * width // 3, rows // 2
    below = start + rows
    out[start:below, :] = value[:, :wide]
    out[below : below + half, : wide // 2] = value[:half, wide:]
    out[below : below + half, wide // 2 :] = value[half:, wide:]


def unfold(value, out, start):
    rows, wide = value.shape[0] * 2 // 3, value.shape[1]
    middle, end = start + rows // 2, start + rows
    out[start:end, :wide] = value[:rows]
    out[start:middle, wide:] = value[rows:, : wide // 2]
    out[middle:end, wide:] = value[rows:, wide // 2 :]


def spline_kernel(src_rows, dst_nodes, counts, weights, modes, pack):
    owners, slots = src_rows.shape[2:]
    dofs, node_count, width = modes.shape
    share = dofs * node_count // lax.axis_size("col")
    sub_rows = (pack.shape[0] - folded(share)) * 2 // 3
    shape = (sub_rows, owners * dofs * node_count)
    row = lax.broadcasted_iota(jnp.int32, shape, 0)
    place = lax.broadcasted_iota(jnp.int32, shape, 1)
    total = jnp.zeros(shape, jnp.float32)
    for owner in range(owners):
        live = counts[0, 0, owner]
        for slot in range(slots):
            node = owner * dofs * node_count + dst_nodes[0, 0, owner, slot]
            term = jnp.zeros(shape, jnp.float32)
            for dof in range(dofs):
                term = jnp.where(place == node + dof * node_count, weights[0, 0, dof, owner, slot], term)
            here = jnp.where(slot < live, src_rows[0, 0, owner, slot], -1)
            total = total + jnp.where(row == here, term, 0.0)
    fold(total, pack, 0)
    flat = modes[...].reshape(dofs * node_count, width)
    col = lax.axis_index("col")
    for turn in range(lax.axis_size("col")):

        @pl.when(col == turn)
        def _():
            fold(flat[turn * share : (turn + 1) * share], pack, folded(sub_rows))


def transfer_kernel(sub_rows, packs, high, low, modes, spread):
    cols, blk_count = packs.shape[:2]
    blk, col = lax.axis_index("blk"), lax.axis_index("col")
    spline_rows = folded(sub_rows)
    share = (packs.shape[2] - spline_rows) * 2 // 3
    half = blk_count // 2
    quarter = cols // 2
    own = blk // half * half
    bits = cols.bit_length() - 1

    def entry(place):
        mask = col ^ place
        return sum(((mask >> bit) & 1) << (bits - 1 - bit) for bit in range(bits))

    for b in range(blk_count):
        for c in range(cols):
            at = (b * cols + c) * share
            unfold(packs[entry(c), blk ^ b, spline_rows:, :], modes, at)
    at = 0
    for turn in range(2):
        for b in range(blk_count):
            block = own + b if b < half else half - own + b - half
            for c in range(quarter):
                place = (lax.rem(col, 2) ^ turn) * quarter + c
                unfold(packs[entry(place), blk ^ block, :spline_rows, :], spread, at)
                at += sub_rows
    whole = lax.dot_general(
        modes[...], spread[...], (((0,), (1,)), ((), ())), precision=HIGHEST,
        preferred_element_type=jnp.float32,
    )
    high[...], low[...] = split(whole)


def last_kernel(high, low, total, other, out):
    right_high, right_low = split(jnp.concatenate([total[...], other[...]]))
    out[...] = mxu(high[...], right_high) + (mxu(high[...], right_low) + mxu(low[...], right_high))


def split(value):
    high = value.astype(jnp.bfloat16)
    return high, (value - high.astype(jnp.float32)).astype(jnp.bfloat16)


def mxu(left, right):
    return jnp.dot(left, right, preferred_element_type=jnp.float32)


def halves_kernel(shapes, high, low, buffer, sems):
    steps = buffer.shape[0]
    rows = buffer.shape[1]
    copies = [
        pltpu.make_async_copy(shapes.at[pl.ds(step * rows, rows), :], buffer.at[step], sems.at[step])
        for step in range(steps)
    ]
    for copy in copies:
        copy.start()
    for step, copy in enumerate(copies):
        copy.wait()
        at = pl.ds(step * rows, rows)
        high[at, :], low[at, :] = split(buffer[step])


def halves(shapes, steps):
    rows = shapes.shape[0] // steps
    return pl.pallas_call(
        halves_kernel,
        out_shape=[jax.ShapeDtypeStruct(shapes.shape, jnp.bfloat16)] * 2,
        in_specs=[ANY],
        out_specs=[VMEM] * 2,
        scratch_shapes=[
            pltpu.VMEM((steps, rows, shapes.shape[1]), jnp.float32),
            pltpu.SemaphoreType.DMA((steps,)),
        ],
        compiler_params=ROOM,
        cost_estimate=cost(0.001),
    )(shapes)


def product(pieces, high, low):
    rows = [split(piece[...]) for piece in pieces]
    left_high = jnp.concatenate([r[0] for r in rows])
    left_low = jnp.concatenate([r[1] for r in rows])
    size = left_high.shape[0]
    both = mxu(jnp.concatenate([left_high, left_low]), high[...])
    return both[:size] + both[size:] + mxu(left_high, low[...])


def early_kernel(*refs):
    *pieces, high, low, out = refs
    out[...] = product(pieces, high, low)


def late_kernel(groups, *refs):
    *pieces, early, high, low, kept, given, total = refs
    done = early.shape[0]
    total[:done, :] = early[...]
    total[done:, :] = product(pieces, high, low)
    blk, core = lax.axis_index("blk"), lax.rem(lax.axis_index("col"), 2)
    rows = total.shape[0] // sum(groups)
    half = rows // 2
    at = first = 0
    for group in groups:
        for index in range(group):
            source = (first + ((blk & (group - 1)) ^ index)) * rows
            for side, out in ((core, kept), (1 - core, given)):
                place = pl.multiple_of(source + side * half, 8)
                out[at : at + half, :] = total[pl.ds(place, half), :]
            at += half
        first += group


def early_products(pieces, high, low):
    return pl.pallas_call(
        early_kernel,
        out_shape=f32(sum(piece.shape[0] for piece in pieces), high.shape[1]),
        in_specs=[VMEM] * (len(pieces) + 2),
        out_specs=VMEM,
        compiler_params=ROOM,
        cost_estimate=cost(0.001),
    )(*pieces, high, low)


def late_products(groups, pieces, early, high, low):
    width = high.shape[1]
    rows = early.shape[0] + sum(piece.shape[0] for piece in pieces)
    return pl.pallas_call(
        functools.partial(late_kernel, groups),
        out_shape=[f32(rows // 2, width)] * 2,
        in_specs=[VMEM] * (len(pieces) + 3),
        out_specs=[VMEM] * 2,
        scratch_shapes=[pltpu.VMEM((rows, width), jnp.float32)],
        compiler_params=ROOM,
        cost_estimate=cost(0.001),
    )(*pieces, early, high, low)


def joined_kernel(*refs):
    *parts, out = refs
    for index, part in enumerate(parts):
        out[index] = part[...]


def joined(*parts):
    return pl.pallas_call(
        joined_kernel,
        out_shape=f32(len(parts), *parts[0].shape),
        in_specs=[VMEM] * len(parts),
        out_specs=VMEM,
        compiler_params=ROOM,
        cost_estimate=cost(0.001),
    )(*parts)


def shards(aic, downwash, node_modes, src_rows, dst_nodes, counts, spline_weights):
    blk_count, col_count = lax.axis_size("blk"), lax.axis_size("col")
    shapes = downwash[0]
    panels, width = shapes.shape
    block_rows = aic.shape[0]
    sub_rows = block_rows // col_count
    dofs, node_count, modes = node_modes.shape
    loads = blk_count * dofs * node_count
    half = blk_count // 2

    share = dofs * node_count // col_count
    blk = lax.axis_index("blk")

    def columns(mask, source=aic):
        return lax.dynamic_slice_in_dim(source, (blk ^ mask) * panels, panels, 1)

    far_masks = list(range(half, blk_count))
    far = [columns(mask) for mask in far_masks[:-1]]
    rest, *far = lax.optimization_barrier((aic, *far))
    far = [swap(piece, "blk", mask) for mask, piece in zip(far_masks, far)]
    near = [columns(mask, rest) for mask in range(1, half)]
    last = columns(far_masks[-1], rest)
    rest, lists, shapes, last, *near = lax.optimization_barrier((rest, src_rows, shapes, last, *near))
    near = [swap(piece, "blk", mask + 1) for mask, piece in enumerate(near)]
    near = [columns(0, rest), *near]
    high, low = halves(shapes, 4)

    pack = pl.pallas_call(
        spline_kernel,
        out_shape=f32(folded(sub_rows) + folded(share), 2 * modes // 3),
        in_specs=[SMEM] * 4 + [VMEM],
        out_specs=VMEM,
        compiler_params=ROOM,
        cost_estimate=cost(0.001),
    )(lists, dst_nodes, counts, spline_weights, node_modes)
    last = swap(last, "blk", far_masks[-1])
    packs = [pack] + [swap(pack, "blk", mask) for mask in range(1, blk_count)]
    waiting = lax.optimization_barrier((*packs[::-1], *near, *far))
    packs, near, far = waiting[:blk_count][::-1], waiting[blk_count : blk_count + half], waiting[blk_count + half :]
    packs = joined(*packs)[None]
    for mask in masks("col")[:0:-1]:
        packs = joined(packs, swap(packs, "col", mask)).reshape(-1, *packs.shape[1:])
    packs, high = lax.optimization_barrier((packs, high))

    early = early_products([*near, *far], high, low)
    total, given = late_products((half, half), [last], early, high, low)
    packs = jnp.concatenate([packs, swap(packs, "col", 1)])
    total = total + swap(given, "col", 1)
    for mask in masks("col")[1:]:
        total = total + swap(total, "col", mask)
    for mask in masks("blk")[:-1]:
        total = total + swap(total, "blk", mask)
    there = swap(total, "blk", half)
    transfer = pl.pallas_call(
        functools.partial(transfer_kernel, sub_rows),
        out_shape=[jax.ShapeDtypeStruct((modes, blk_count * block_rows), jnp.bfloat16)] * 2,
        in_specs=[VMEM],
        out_specs=[VMEM] * 2,
        scratch_shapes=[
            pltpu.VMEM((loads, modes), jnp.float32),
            pltpu.VMEM((blk_count * block_rows, loads), jnp.float32),
        ],
        compiler_params=ROOM,
        cost_estimate=cost(3),
    )(packs)
    there, *transfer = lax.optimization_barrier((there, *transfer))
    rows = total.shape[0] // 2
    total = total + jnp.concatenate([there[rows:], there[:rows]])
    other = swap(total, "col", 1)
    return pl.pallas_call(
        last_kernel,
        out_shape=f32(modes, width),
        compiler_params=ROOM,
    )(*transfer, total, other)


def solution(mesh):
    placed = (
        P(("groups", "blk"), "col"),
        P(("groups", "col"), "blk", None),
        P(None, "blk", None),
        P("blk", "col", None, None),
        P("blk", "col", None, None),
        P("blk", "col", None),
        P("blk", "col", None, None, None),
    )

    def program(*arrays):
        dofs, nodes, modes = arrays[2].shape
        blk_count, col_count = mesh.shape["blk"], mesh.shape["col"]
        small = dofs * nodes == modes and modes % 3 == 0
        body = shards if small and blk_count > 2 and col_count > 2 else by_parts
        return jax.shard_map(
            body, mesh=mesh, in_specs=placed, out_specs=P("groups", None), check_vma=False
        )(*arrays)

    return program
```

```python
import functools

import jax
import jax.numpy as jnp
from jax import lax
from jax.experimental import pallas as pl
from jax.experimental.pallas import tpu as pltpu
from jax.sharding import PartitionSpec as P

HIGH = lax.Precision.HIGH
HIGHEST = lax.Precision.HIGHEST
VMEM = pl.BlockSpec(memory_space=pltpu.VMEM)
SMEM = pl.BlockSpec(memory_space=pltpu.SMEM)
ANY = pl.BlockSpec(memory_space=pl.ANY)
ROOM = pltpu.CompilerParams(vmem_limit_bytes=32 * 1024 * 1024)


def swap(value, axis, mask):
    pairs = [(source, source ^ mask) for source in range(lax.axis_size(axis))]
    return lax.ppermute(value, axis, pairs)


def masks(axis):
    count, mask, found = lax.axis_size(axis), 1, []
    while mask < count:
        found.append(mask)
        mask *= 2
    return found


def gathered(value, axis):
    stack = value[None]
    for mask in masks(axis):
        stack = jnp.concatenate([stack, swap(stack, axis, mask)])
    return stack


def dot(left, right):
    return jnp.dot(left, right, precision=HIGH, preferred_element_type=jnp.float32)


def spline(src_rows, dst_nodes, counts, weights, sub_rows, node_count):
    slots = src_rows.shape[-1]
    live = jnp.arange(slots, dtype=jnp.int32) < counts[:, None]
    rows = jnp.arange(sub_rows, dtype=jnp.int32)[:, None, None] == src_rows
    rows = jnp.logical_and(rows, live).astype(jnp.float32)
    nodes = jnp.arange(node_count, dtype=jnp.int32)[:, None, None] == dst_nodes
    spread = weights[:, None] * nodes.astype(jnp.float32)
    matrix = jnp.sum(rows[:, None, None] * spread, axis=-1)
    return jnp.transpose(matrix, (0, 3, 1, 2)).reshape(sub_rows, -1)


def by_parts(aic, downwash, node_modes, src_rows, dst_nodes, counts, spline_weights):
    blk_count, col_count = lax.axis_size("blk"), lax.axis_size("col")
    blk, col = lax.axis_index("blk"), lax.axis_index("col")
    shapes = downwash[0]
    panels = shapes.shape[0]
    block_rows = aic.shape[0]
    sub_rows = block_rows // col_count
    dofs, node_count, modes = node_modes.shape

    def columns(mask):
        return lax.dynamic_slice_in_dim(aic, (blk ^ mask) * panels, panels, 1)

    order = sorted(range(1, blk_count), key=lambda mask: (mask < blk_count // 2, mask))
    arrived = {mask: swap(columns(mask), "blk", mask) for mask in order}
    arrived[0] = columns(0)
    pieces = jnp.stack([dot(arrived[mask], shapes) for mask in range(blk_count)])

    matrix = spline(
        src_rows[0, 0], dst_nodes[0, 0], counts[0, 0], spline_weights[0, 0], sub_rows, node_count
    )
    flat_modes = node_modes.reshape(dofs * node_count, modes)
    share = dofs * node_count // col_count
    modes_share = lax.dynamic_slice_in_dim(flat_modes, col * share, share, 0)
    natural_blk = blk ^ jnp.arange(blk_count, dtype=jnp.int32)
    natural_col = col ^ jnp.arange(col_count, dtype=jnp.int32)

    def everywhere(value):
        stack = gathered(gathered(value, "blk"), "col")
        return jnp.swapaxes(stack[natural_col], 0, 1)

    if matrix.shape[1] == modes:
        packed = everywhere(jnp.concatenate([modes_share, matrix]))
        all_modes = packed[natural_blk, :, :share].reshape(-1, modes)
        transfer = dot(packed[:, :, share:].reshape(-1, modes), all_modes)
    else:
        all_modes = everywhere(modes_share)[natural_blk].reshape(-1, modes)
        transfer = everywhere(dot(matrix, all_modes)).reshape(-1, modes)
    transfer = transfer.reshape(blk_count, block_rows, modes)

    half = block_rows // 2
    side = col % 2
    kept = lax.dynamic_slice_in_dim(pieces, side * half, half, 1)
    given = lax.dynamic_slice_in_dim(pieces, (1 - side) * half, half, 1)
    kept = kept + swap(given, "col", 1)
    for mask in masks("col")[1:]:
        kept = kept + swap(kept, "col", mask)
    for mask in masks("blk"):
        turned = kept[jnp.arange(blk_count) ^ mask]
        kept = kept + swap(turned, "blk", mask)
    other = swap(kept, "col", 1)
    first = lax.dynamic_slice_in_dim(transfer, side * half, half, 1)
    second = lax.dynamic_slice_in_dim(transfer, (1 - side) * half, half, 1)
    width = shapes.shape[1]
    return dot(first.reshape(-1, modes).T, kept.reshape(-1, width)) + dot(
        second.reshape(-1, modes).T, other.reshape(-1, width)
    )


def cost(microseconds):
    return pl.CostEstimate(flops=0, bytes_accessed=int(microseconds * 3.5e6), transcendentals=0)


def after(value, *others):
    return lax.optimization_barrier((value, *others))[0]


def f32(*shape):
    return jax.ShapeDtypeStruct(shape, jnp.float32)


def folded(rows):
    return rows + rows // 2


def fold(value, out, start):
    rows, width = value.shape
    wide, half = 2 * width // 3, rows // 2
    below = start + rows
    out[start:below, :] = value[:, :wide]
    out[below : below + half, : wide // 2] = value[:half, wide:]
    out[below : below + half, wide // 2 :] = value[half:, wide:]


def unfold(value, out, start):
    rows, wide = value.shape[0] * 2 // 3, value.shape[1]
    middle, end = start + rows // 2, start + rows
    out[start:end, :wide] = value[:rows]
    out[start:middle, wide:] = value[rows:, : wide // 2]
    out[middle:end, wide:] = value[rows:, wide // 2 :]


def spline_kernel(src_rows, dst_nodes, counts, weights, modes, pack):
    owners, slots = src_rows.shape[2:]
    dofs, node_count, width = modes.shape
    share = dofs * node_count // lax.axis_size("col")
    sub_rows = (pack.shape[0] - folded(share)) * 2 // 3
    shape = (sub_rows, owners * dofs * node_count)
    row = lax.broadcasted_iota(jnp.int32, shape, 0)
    place = lax.broadcasted_iota(jnp.int32, shape, 1)
    total = jnp.zeros(shape, jnp.float32)
    for owner in range(owners):
        live = counts[0, 0, owner]
        for slot in range(slots):
            node = owner * dofs * node_count + dst_nodes[0, 0, owner, slot]
            term = jnp.zeros(shape, jnp.float32)
            for dof in range(dofs):
                term = jnp.where(place == node + dof * node_count, weights[0, 0, dof, owner, slot], term)
            here = jnp.where(slot < live, src_rows[0, 0, owner, slot], -1)
            total = total + jnp.where(row == here, term, 0.0)
    fold(total, pack, 0)
    flat = modes[...].reshape(dofs * node_count, width)
    col = lax.axis_index("col")
    for turn in range(lax.axis_size("col")):

        @pl.when(col == turn)
        def _():
            fold(flat[turn * share : (turn + 1) * share], pack, folded(sub_rows))


def transfer_kernel(sub_rows, packs, high, low, modes, spread):
    cols, blk_count = packs.shape[:2]
    blk, col = lax.axis_index("blk"), lax.axis_index("col")
    spline_rows = folded(sub_rows)
    share = (packs.shape[2] - spline_rows) * 2 // 3
    half = blk_count // 2
    quarter = cols // 2
    own = blk // half * half
    bits = cols.bit_length() - 1

    def entry(place):
        mask = col ^ place
        return sum(((mask >> bit) & 1) << (bits - 1 - bit) for bit in range(bits))

    for b in range(blk_count):
        for c in range(cols):
            at = (b * cols + c) * share
            unfold(packs[entry(c), blk ^ b, spline_rows:, :], modes, at)
    at = 0
    for turn in range(2):
        for b in range(blk_count):
            block = own + b if b < half else half - own + b - half
            for c in range(quarter):
                place = (lax.rem(col, 2) ^ turn) * quarter + c
                unfold(packs[entry(place), blk ^ block, :spline_rows, :], spread, at)
                at += sub_rows
    whole = lax.dot_general(
        modes[...], spread[...], (((0,), (1,)), ((), ())), precision=HIGHEST,
        preferred_element_type=jnp.float32,
    )
    high[...], low[...] = split(whole)


def modal(high, low, rows):
    right_high, right_low = split(rows[...])
    return mxu(high, right_high) + (mxu(high, right_low) + mxu(low, right_high))


def base_kernel(high, low, total, out):
    count = total.shape[0]
    out[...] = modal(high[:, :count], low[:, :count], total)


def last_kernel(high, low, base, other, out):
    count = other.shape[0]
    out[...] = base[...] + modal(high[:, count:], low[:, count:], other)


def split(value):
    high = value.astype(jnp.bfloat16)
    return high, (value - high.astype(jnp.float32)).astype(jnp.bfloat16)


def mxu(left, right):
    return jnp.dot(left, right, preferred_element_type=jnp.float32)


def halves_kernel(shapes, high, low, buffer, sems):
    steps = buffer.shape[0]
    rows = buffer.shape[1]
    copies = [
        pltpu.make_async_copy(shapes.at[pl.ds(step * rows, rows), :], buffer.at[step], sems.at[step])
        for step in range(steps)
    ]
    for copy in copies:
        copy.start()
    for step, copy in enumerate(copies):
        copy.wait()
        at = pl.ds(step * rows, rows)
        high[at, :], low[at, :] = split(buffer[step])


def halves(shapes, steps):
    rows = shapes.shape[0] // steps
    return pl.pallas_call(
        halves_kernel,
        out_shape=[jax.ShapeDtypeStruct(shapes.shape, jnp.bfloat16)] * 2,
        in_specs=[ANY],
        out_specs=[VMEM] * 2,
        scratch_shapes=[
            pltpu.VMEM((steps, rows, shapes.shape[1]), jnp.float32),
            pltpu.SemaphoreType.DMA((steps,)),
        ],
        compiler_params=ROOM,
        cost_estimate=cost(0.001),
    )(shapes)


def product(pieces, high, low):
    rows = [split(piece[...]) for piece in pieces]
    left_high = jnp.concatenate([r[0] for r in rows])
    left_low = jnp.concatenate([r[1] for r in rows])
    size = left_high.shape[0]
    both = mxu(jnp.concatenate([left_high, left_low]), high[...])
    return both[:size] + both[size:] + mxu(left_high, low[...])


def early_kernel(*refs):
    *pieces, high, low, out = refs
    out[...] = product(pieces, high, low)


def late_kernel(groups, *refs):
    *pieces, early, high, low, kept, given, total = refs
    done = early.shape[0]
    total[:done, :] = early[...]
    total[done:, :] = product(pieces, high, low)
    blk, core = lax.axis_index("blk"), lax.rem(lax.axis_index("col"), 2)
    rows = total.shape[0] // sum(groups)
    half = rows // 2
    at = first = 0
    for group in groups:
        for index in range(group):
            source = (first + ((blk & (group - 1)) ^ index)) * rows
            for side, out in ((core, kept), (1 - core, given)):
                place = pl.multiple_of(source + side * half, 8)
                out[at : at + half, :] = total[pl.ds(place, half), :]
            at += half
        first += group


def early_products(pieces, high, low):
    return pl.pallas_call(
        early_kernel,
        out_shape=f32(sum(piece.shape[0] for piece in pieces), high.shape[1]),
        in_specs=[VMEM] * (len(pieces) + 2),
        out_specs=VMEM,
        compiler_params=ROOM,
        cost_estimate=cost(0.001),
    )(*pieces, high, low)


def late_products(groups, pieces, early, high, low):
    width = high.shape[1]
    rows = early.shape[0] + sum(piece.shape[0] for piece in pieces)
    return pl.pallas_call(
        functools.partial(late_kernel, groups),
        out_shape=[f32(rows // 2, width)] * 2,
        in_specs=[VMEM] * (len(pieces) + 3),
        out_specs=[VMEM] * 2,
        scratch_shapes=[pltpu.VMEM((rows, width), jnp.float32)],
        compiler_params=ROOM,
        cost_estimate=cost(0.001),
    )(*pieces, early, high, low)


def joined_kernel(*refs):
    *parts, out = refs
    for index, part in enumerate(parts):
        out[index] = part[...]


def joined(*parts):
    return pl.pallas_call(
        joined_kernel,
        out_shape=f32(len(parts), *parts[0].shape),
        in_specs=[VMEM] * len(parts),
        out_specs=VMEM,
        compiler_params=ROOM,
        cost_estimate=cost(0.001),
    )(*parts)


def shards(aic, downwash, node_modes, src_rows, dst_nodes, counts, spline_weights):
    blk_count, col_count = lax.axis_size("blk"), lax.axis_size("col")
    shapes = downwash[0]
    panels, width = shapes.shape
    block_rows = aic.shape[0]
    sub_rows = block_rows // col_count
    dofs, node_count, modes = node_modes.shape
    loads = blk_count * dofs * node_count
    half = blk_count // 2

    share = dofs * node_count // col_count
    blk = lax.axis_index("blk")

    def columns(mask, source=aic):
        return lax.dynamic_slice_in_dim(source, (blk ^ mask) * panels, panels, 1)

    far_masks = list(range(half, blk_count))
    far = [columns(mask) for mask in far_masks[:-1]]
    rest, *far = lax.optimization_barrier((aic, *far))
    far = [swap(piece, "blk", mask) for mask, piece in zip(far_masks, far)]
    near = [columns(mask, rest) for mask in range(1, half)]
    last = columns(far_masks[-1], rest)
    rest, lists, shapes, last, *near = lax.optimization_barrier((rest, src_rows, shapes, last, *near))
    near = [swap(piece, "blk", mask + 1) for mask, piece in enumerate(near)]
    near = [columns(0, rest), *near]
    high, low = halves(shapes, 4)

    pack = pl.pallas_call(
        spline_kernel,
        out_shape=f32(folded(sub_rows) + folded(share), 2 * modes // 3),
        in_specs=[SMEM] * 4 + [VMEM],
        out_specs=VMEM,
        compiler_params=ROOM,
        cost_estimate=cost(0.001),
    )(lists, dst_nodes, counts, spline_weights, node_modes)
    last = swap(last, "blk", far_masks[-1])
    packs = [pack] + [swap(pack, "blk", mask) for mask in range(1, blk_count)]
    waiting = lax.optimization_barrier((*packs[::-1], *near, *far))
    packs, near, far = waiting[:blk_count][::-1], waiting[blk_count : blk_count + half], waiting[blk_count + half :]
    packs = joined(*packs)[None]
    for mask in masks("col")[:0:-1]:
        packs = joined(packs, swap(packs, "col", mask)).reshape(-1, *packs.shape[1:])
    packs, high = lax.optimization_barrier((packs, high))

    early = early_products([*near, *far], high, low)
    total, given = late_products((half, half), [last], early, high, low)
    packs = jnp.concatenate([packs, swap(packs, "col", 1)])
    total = total + swap(given, "col", 1)
    for mask in masks("col")[1:]:
        total = total + swap(total, "col", mask)
    for mask in masks("blk")[:-1]:
        total = total + swap(total, "blk", mask)
    there = swap(total, "blk", half)
    transfer = pl.pallas_call(
        functools.partial(transfer_kernel, sub_rows),
        out_shape=[jax.ShapeDtypeStruct((modes, blk_count * block_rows), jnp.bfloat16)] * 2,
        in_specs=[VMEM],
        out_specs=[VMEM] * 2,
        scratch_shapes=[
            pltpu.VMEM((loads, modes), jnp.float32),
            pltpu.VMEM((blk_count * block_rows, loads), jnp.float32),
        ],
        compiler_params=ROOM,
        cost_estimate=cost(3),
    )(packs)
    there, *transfer = lax.optimization_barrier((there, *transfer))
    rows = total.shape[0] // 2
    total = total + jnp.concatenate([there[rows:], there[:rows]])
    other = swap(total, "col", 1)
    base = pl.pallas_call(
        base_kernel,
        out_shape=f32(modes, width),
        in_specs=[VMEM] * 3,
        out_specs=VMEM,
        compiler_params=ROOM,
        cost_estimate=cost(1),
    )(*transfer, total)
    return pl.pallas_call(
        last_kernel,
        out_shape=f32(modes, width),
        in_specs=[VMEM] * 4,
        compiler_params=ROOM,
    )(*transfer, base, other)


def solution(mesh):
    placed = (
        P(("groups", "blk"), "col"),
        P(("groups", "col"), "blk", None),
        P(None, "blk", None),
        P("blk", "col", None, None),
        P("blk", "col", None, None),
        P("blk", "col", None),
        P("blk", "col", None, None, None),
    )

    def program(*arrays):
        dofs, nodes, modes = arrays[2].shape
        blk_count, col_count = mesh.shape["blk"], mesh.shape["col"]
        small = dofs * nodes == modes and modes % 3 == 0
        body = shards if small and blk_count > 2 and col_count > 2 else by_parts
        return jax.shard_map(
            body, mesh=mesh, in_specs=placed, out_specs=P("groups", None), check_vma=False
        )(*arrays)

    return program
```

```python
import functools

import jax
import jax.numpy as jnp
from jax import lax
from jax.experimental import pallas as pl
from jax.experimental.pallas import tpu as pltpu
from jax.sharding import PartitionSpec as P

HIGH = lax.Precision.HIGH
HIGHEST = lax.Precision.HIGHEST
VMEM = pl.BlockSpec(memory_space=pltpu.VMEM)
SMEM = pl.BlockSpec(memory_space=pltpu.SMEM)
ANY = pl.BlockSpec(memory_space=pl.ANY)
ROOM = pltpu.CompilerParams(vmem_limit_bytes=32 * 1024 * 1024)


def swap(value, axis, mask):
    pairs = [(source, source ^ mask) for source in range(lax.axis_size(axis))]
    return lax.ppermute(value, axis, pairs)


def masks(axis):
    count, mask, found = lax.axis_size(axis), 1, []
    while mask < count:
        found.append(mask)
        mask *= 2
    return found


def gathered(value, axis):
    stack = value[None]
    for mask in masks(axis):
        stack = jnp.concatenate([stack, swap(stack, axis, mask)])
    return stack


def dot(left, right):
    return jnp.dot(left, right, precision=HIGH, preferred_element_type=jnp.float32)


def spline(src_rows, dst_nodes, counts, weights, sub_rows, node_count):
    slots = src_rows.shape[-1]
    live = jnp.arange(slots, dtype=jnp.int32) < counts[:, None]
    rows = jnp.arange(sub_rows, dtype=jnp.int32)[:, None, None] == src_rows
    rows = jnp.logical_and(rows, live).astype(jnp.float32)
    nodes = jnp.arange(node_count, dtype=jnp.int32)[:, None, None] == dst_nodes
    spread = weights[:, None] * nodes.astype(jnp.float32)
    matrix = jnp.sum(rows[:, None, None] * spread, axis=-1)
    return jnp.transpose(matrix, (0, 3, 1, 2)).reshape(sub_rows, -1)


def by_parts(aic, downwash, node_modes, src_rows, dst_nodes, counts, spline_weights):
    blk_count, col_count = lax.axis_size("blk"), lax.axis_size("col")
    blk, col = lax.axis_index("blk"), lax.axis_index("col")
    shapes = downwash[0]
    panels = shapes.shape[0]
    block_rows = aic.shape[0]
    sub_rows = block_rows // col_count
    dofs, node_count, modes = node_modes.shape

    def columns(mask):
        return lax.dynamic_slice_in_dim(aic, (blk ^ mask) * panels, panels, 1)

    order = sorted(range(1, blk_count), key=lambda mask: (mask < blk_count // 2, mask))
    arrived = {mask: swap(columns(mask), "blk", mask) for mask in order}
    arrived[0] = columns(0)
    pieces = jnp.stack([dot(arrived[mask], shapes) for mask in range(blk_count)])

    matrix = spline(
        src_rows[0, 0], dst_nodes[0, 0], counts[0, 0], spline_weights[0, 0], sub_rows, node_count
    )
    flat_modes = node_modes.reshape(dofs * node_count, modes)
    share = dofs * node_count // col_count
    modes_share = lax.dynamic_slice_in_dim(flat_modes, col * share, share, 0)
    natural_blk = blk ^ jnp.arange(blk_count, dtype=jnp.int32)
    natural_col = col ^ jnp.arange(col_count, dtype=jnp.int32)

    def everywhere(value):
        stack = gathered(gathered(value, "blk"), "col")
        return jnp.swapaxes(stack[natural_col], 0, 1)

    if matrix.shape[1] == modes:
        packed = everywhere(jnp.concatenate([modes_share, matrix]))
        all_modes = packed[natural_blk, :, :share].reshape(-1, modes)
        transfer = dot(packed[:, :, share:].reshape(-1, modes), all_modes)
    else:
        all_modes = everywhere(modes_share)[natural_blk].reshape(-1, modes)
        transfer = everywhere(dot(matrix, all_modes)).reshape(-1, modes)
    transfer = transfer.reshape(blk_count, block_rows, modes)

    half = block_rows // 2
    side = col % 2
    kept = lax.dynamic_slice_in_dim(pieces, side * half, half, 1)
    given = lax.dynamic_slice_in_dim(pieces, (1 - side) * half, half, 1)
    kept = kept + swap(given, "col", 1)
    for mask in masks("col")[1:]:
        kept = kept + swap(kept, "col", mask)
    for mask in masks("blk"):
        turned = kept[jnp.arange(blk_count) ^ mask]
        kept = kept + swap(turned, "blk", mask)
    other = swap(kept, "col", 1)
    first = lax.dynamic_slice_in_dim(transfer, side * half, half, 1)
    second = lax.dynamic_slice_in_dim(transfer, (1 - side) * half, half, 1)
    width = shapes.shape[1]
    return dot(first.reshape(-1, modes).T, kept.reshape(-1, width)) + dot(
        second.reshape(-1, modes).T, other.reshape(-1, width)
    )


def cost(microseconds):
    return pl.CostEstimate(flops=0, bytes_accessed=int(microseconds * 3.5e6), transcendentals=0)


def after(value, *others):
    return lax.optimization_barrier((value, *others))[0]


def f32(*shape):
    return jax.ShapeDtypeStruct(shape, jnp.float32)


def folded(rows):
    return rows + rows // 2


def fold(value, out, start):
    rows, width = value.shape
    wide, half = 2 * width // 3, rows // 2
    below = start + rows
    out[start:below, :] = value[:, :wide]
    out[below : below + half, : wide // 2] = value[:half, wide:]
    out[below : below + half, wide // 2 :] = value[half:, wide:]


def unfold(value, out, start):
    rows, wide = value.shape[0] * 2 // 3, value.shape[1]
    middle, end = start + rows // 2, start + rows
    out[start:end, :wide] = value[:rows]
    out[start:middle, wide:] = value[rows:, : wide // 2]
    out[middle:end, wide:] = value[rows:, wide // 2 :]


def spline_kernel(src_rows, dst_nodes, counts, weights, modes, pack):
    owners, slots = src_rows.shape[2:]
    dofs, node_count, width = modes.shape
    share = dofs * node_count // lax.axis_size("col")
    sub_rows = (pack.shape[0] - folded(share)) * 2 // 3
    shape = (sub_rows, owners * dofs * node_count)
    row = lax.broadcasted_iota(jnp.int32, shape, 0)
    place = lax.broadcasted_iota(jnp.int32, shape, 1)
    total = jnp.zeros(shape, jnp.float32)
    for owner in range(owners):
        live = counts[0, 0, owner]
        for slot in range(slots):
            node = owner * dofs * node_count + dst_nodes[0, 0, owner, slot]
            term = jnp.zeros(shape, jnp.float32)
            for dof in range(dofs):
                term = jnp.where(place == node + dof * node_count, weights[0, 0, dof, owner, slot], term)
            here = jnp.where(slot < live, src_rows[0, 0, owner, slot], -1)
            total = total + jnp.where(row == here, term, 0.0)
    fold(total, pack, 0)
    flat = modes[...].reshape(dofs * node_count, width)
    col = lax.axis_index("col")
    for turn in range(lax.axis_size("col")):

        @pl.when(col == turn)
        def _():
            fold(flat[turn * share : (turn + 1) * share], pack, folded(sub_rows))


def transfer_kernel(sub_rows, packs, high, low, modes, spread):
    cols, blk_count = packs.shape[:2]
    blk, col = lax.axis_index("blk"), lax.axis_index("col")
    spline_rows = folded(sub_rows)
    share = (packs.shape[2] - spline_rows) * 2 // 3
    half = blk_count // 2
    quarter = cols // 2
    own = blk // half * half
    bits = cols.bit_length() - 1

    def entry(place):
        mask = col ^ place
        return sum(((mask >> bit) & 1) << (bits - 1 - bit) for bit in range(bits))

    for b in range(blk_count):
        for c in range(cols):
            at = (b * cols + c) * share
            unfold(packs[entry(c), blk ^ b, spline_rows:, :], modes, at)
    at = 0
    for turn in range(2):
        for b in range(blk_count):
            block = own + b if b < half else half - own + b - half
            for c in range(quarter):
                place = (lax.rem(col, 2) ^ turn) * quarter + c
                unfold(packs[entry(place), blk ^ block, :spline_rows, :], spread, at)
                at += sub_rows
    whole = lax.dot_general(
        modes[...], spread[...], (((0,), (1,)), ((), ())), precision=HIGHEST,
        preferred_element_type=jnp.float32,
    )
    high[...], low[...] = split(whole)


def last_kernel(high, low, total, other, out):
    right_high, right_low = split(jnp.concatenate([total[...], other[...]]))
    out[...] = mxu(high[...], right_high) + (mxu(high[...], right_low) + mxu(low[...], right_high))


def split(value):
    high = value.astype(jnp.bfloat16)
    return high, (value - high.astype(jnp.float32)).astype(jnp.bfloat16)


def mxu(left, right):
    return jnp.dot(left, right, preferred_element_type=jnp.float32)


def halves_kernel(shapes, high, low, buffer, sems):
    steps = buffer.shape[0]
    rows = buffer.shape[1]
    copies = [
        pltpu.make_async_copy(shapes.at[pl.ds(step * rows, rows), :], buffer.at[step], sems.at[step])
        for step in range(steps)
    ]
    for copy in copies:
        copy.start()
    for step, copy in enumerate(copies):
        copy.wait()
        at = pl.ds(step * rows, rows)
        high[at, :], low[at, :] = split(buffer[step])


def halves(shapes, steps):
    rows = shapes.shape[0] // steps
    return pl.pallas_call(
        halves_kernel,
        out_shape=[jax.ShapeDtypeStruct(shapes.shape, jnp.bfloat16)] * 2,
        in_specs=[ANY],
        out_specs=[VMEM] * 2,
        scratch_shapes=[
            pltpu.VMEM((steps, rows, shapes.shape[1]), jnp.float32),
            pltpu.SemaphoreType.DMA((steps,)),
        ],
        compiler_params=ROOM,
        cost_estimate=cost(0.001),
    )(shapes)


def product(pieces, high, low):
    rows = [split(piece[...]) for piece in pieces]
    left_high = jnp.concatenate([r[0] for r in rows])
    left_low = jnp.concatenate([r[1] for r in rows])
    size = left_high.shape[0]
    both = mxu(jnp.concatenate([left_high, left_low]), high[...])
    return both[:size] + both[size:] + mxu(left_high, low[...])


def early_kernel(*refs):
    *pieces, high, low, out = refs
    out[...] = product(pieces, high, low)


def late_kernel(groups, *refs):
    *pieces, early, high, low, kept, given, total = refs
    done = early.shape[0]
    total[:done, :] = early[...]
    total[done:, :] = product(pieces, high, low)
    blk, core = lax.axis_index("blk"), lax.rem(lax.axis_index("col"), 2)
    rows = total.shape[0] // sum(groups)
    half = rows // 2
    at = first = 0
    for group in groups:
        for index in range(group):
            source = (first + ((blk & (group - 1)) ^ index)) * rows
            for side, out in ((core, kept), (1 - core, given)):
                place = pl.multiple_of(source + side * half, 8)
                out[at : at + half, :] = total[pl.ds(place, half), :]
            at += half
        first += group


def early_products(pieces, high, low):
    return pl.pallas_call(
        early_kernel,
        out_shape=f32(sum(piece.shape[0] for piece in pieces), high.shape[1]),
        in_specs=[VMEM] * (len(pieces) + 2),
        out_specs=VMEM,
        compiler_params=ROOM,
        cost_estimate=cost(0.001),
    )(*pieces, high, low)


def late_products(groups, pieces, early, high, low):
    width = high.shape[1]
    rows = early.shape[0] + sum(piece.shape[0] for piece in pieces)
    return pl.pallas_call(
        functools.partial(late_kernel, groups),
        out_shape=[f32(rows // 2, width)] * 2,
        in_specs=[VMEM] * (len(pieces) + 3),
        out_specs=[VMEM] * 2,
        scratch_shapes=[pltpu.VMEM((rows, width), jnp.float32)],
        compiler_params=ROOM,
        cost_estimate=cost(0.001),
    )(*pieces, early, high, low)


def joined_kernel(*refs):
    *parts, out = refs
    for index, part in enumerate(parts):
        out[index] = part[...]


def joined(*parts):
    return pl.pallas_call(
        joined_kernel,
        out_shape=f32(len(parts), *parts[0].shape),
        in_specs=[VMEM] * len(parts),
        out_specs=VMEM,
        compiler_params=ROOM,
        cost_estimate=cost(0.001),
    )(*parts)


def shards(aic, downwash, node_modes, src_rows, dst_nodes, counts, spline_weights):
    blk_count, col_count = lax.axis_size("blk"), lax.axis_size("col")
    shapes = downwash[0]
    panels, width = shapes.shape
    block_rows = aic.shape[0]
    sub_rows = block_rows // col_count
    dofs, node_count, modes = node_modes.shape
    loads = blk_count * dofs * node_count
    half = blk_count // 2

    share = dofs * node_count // col_count
    blk = lax.axis_index("blk")

    def columns(mask, source=aic):
        return lax.dynamic_slice_in_dim(source, (blk ^ mask) * panels, panels, 1)

    far_masks = list(range(half, blk_count))
    far = [columns(mask) for mask in far_masks[:-1]]
    rest, *far = lax.optimization_barrier((aic, *far))
    far = [swap(piece, "blk", mask) for mask, piece in zip(far_masks, far)]
    near = [columns(mask, rest) for mask in range(1, half)]
    last = columns(far_masks[-1], rest)
    rest, lists, shapes, last, *near = lax.optimization_barrier((rest, src_rows, shapes, last, *near))
    near = [swap(piece, "blk", mask + 1) for mask, piece in enumerate(near)]
    near = [columns(0, rest), *near]
    high, low = halves(shapes, 4)

    pack = pl.pallas_call(
        spline_kernel,
        out_shape=f32(folded(sub_rows) + folded(share), 2 * modes // 3),
        in_specs=[SMEM] * 4 + [VMEM],
        out_specs=VMEM,
        compiler_params=ROOM,
        cost_estimate=cost(0.001),
    )(lists, dst_nodes, counts, spline_weights, node_modes)
    last = swap(last, "blk", far_masks[-1])
    packs = [pack] + [swap(pack, "blk", mask) for mask in range(1, blk_count)]
    order = [2, 3, 1, 0]
    waiting = lax.optimization_barrier((*[packs[mask] for mask in order], *near, *far))
    packs = [waiting[order.index(mask)] for mask in range(blk_count)]
    near, far = waiting[blk_count : blk_count + half], waiting[blk_count + half :]
    packs = joined(*packs)[None]
    for mask in masks("col")[:0:-1]:
        packs = joined(packs, swap(packs, "col", mask)).reshape(-1, *packs.shape[1:])
    packs, high = lax.optimization_barrier((packs, high))

    early = early_products([*near, *far], high, low)
    total, given = late_products((half, half), [last], early, high, low)
    packs = jnp.concatenate([packs, swap(packs, "col", 1)])
    total = total + swap(given, "col", 1)
    for mask in masks("col")[1:]:
        total = total + swap(total, "col", mask)
    for mask in masks("blk")[:-1]:
        total = total + swap(total, "blk", mask)
    there = swap(total, "blk", half)
    transfer = pl.pallas_call(
        functools.partial(transfer_kernel, sub_rows),
        out_shape=[jax.ShapeDtypeStruct((modes, blk_count * block_rows), jnp.bfloat16)] * 2,
        in_specs=[VMEM],
        out_specs=[VMEM] * 2,
        scratch_shapes=[
            pltpu.VMEM((loads, modes), jnp.float32),
            pltpu.VMEM((blk_count * block_rows, loads), jnp.float32),
        ],
        compiler_params=ROOM,
        cost_estimate=cost(3),
    )(packs)
    there, *transfer = lax.optimization_barrier((there, *transfer))
    rows = total.shape[0] // 2
    total = total + jnp.concatenate([there[rows:], there[:rows]])
    other = swap(total, "col", 1)
    return pl.pallas_call(
        last_kernel,
        out_shape=f32(modes, width),
        compiler_params=ROOM,
    )(*transfer, total, other)


def solution(mesh):
    placed = (
        P(("groups", "blk"), "col"),
        P(("groups", "col"), "blk", None),
        P(None, "blk", None),
        P("blk", "col", None, None),
        P("blk", "col", None, None),
        P("blk", "col", None),
        P("blk", "col", None, None, None),
    )

    def program(*arrays):
        dofs, nodes, modes = arrays[2].shape
        blk_count, col_count = mesh.shape["blk"], mesh.shape["col"]
        small = dofs * nodes == modes and modes % 3 == 0
        body = shards if small and blk_count > 2 and col_count > 2 else by_parts
        return jax.shard_map(
            body, mesh=mesh, in_specs=placed, out_specs=P("groups", None), check_vma=False
        )(*arrays)

    return program
```
